256 devices in a mesh: replica: 16 (over x, z_hi, core), shard: 16 (over z_lo, y).
Axes of the slice: x: 4, y: 4, z: 8 (z_hi: 2, z_lo: 4; z = z_hi * 4 + z_lo), core: 2. Of those that a mesh axis runs over, the one named last changes fastest.
Arguments:
- tokens: bfloat16 [131072, 4096], P(('replica', 'shard')), may hold values from -6 to 6
- cotangent: bfloat16 [131072, 1792], P(('replica', 'shard')), may hold values from -6 to 6
- pseudo_grad: bfloat16 [16, 4096, 1792], P('replica', 'shard'), may hold values from -6 to 6
- anchor: float32 [4096, 1792], P(('shard', 'replica')), may hold values from -6 to 6
- momentum: float32 [4096, 1792], P(('shard', 'replica')), may hold values from -6 to 6
Outputs:
- new_anchor: float32 [4096, 1792], P(('shard', 'replica'))
- new_momentum: float32 [4096, 1792], P(('shard', 'replica'))
- up_acts: bfloat16 [131072, 1792], P(('replica', 'shard'))
- weight_grad: bfloat16 [16, 4096, 1792], P('replica', 'shard')
The draws below stay inside these ranges and needn't reach their ends.
All inputs are finite; a program needn't handle non-finite values.
Results may differ from the reference program's by a relative error of at most 0.0049.
Values may be sent and summed in bfloat16 or wider, within the bound.
No kernel may reach another device: no remote copies, remote signals or barrier semaphores. Data moves between devices by JAX's collectives and lax.ppermute only.
A program may use at most 128 MiB of HBM per device.

```python
import jax
import jax.numpy as jnp
from jax import lax

D = 4096
FF = 1792
TOK_DEV = 512
REPLICAS = 16
SHARDS = 16
TOKENS = 131072


def strengthened(drawn, rng, source, target, shards_of, factor):
    def block_of(position):
        return (jnp.arange(drawn.shape[position]) // (drawn.shape[position] // shards_of)).reshape((-1,) + (1,) * (drawn.ndim - 1 - position))

    first = jax.random.permutation(rng, shards_of)[block_of(target)]
    second = (block_of(target) + shards_of // 2) % shards_of
    return jnp.where((block_of(source) == first) | (block_of(source) == second), factor * drawn, drawn)


def shard_levels(stream_key, extent, split, low, largest):
    factor_of, own = 1.0, jax.random.fold_in(stream_key, 6)
    for axis_at, parts in split:
        draws = jnp.exp(jax.random.uniform(jax.random.fold_in(own, axis_at), (parts,), jnp.float32, low / len(split), largest / len(split)))
        factor_of = factor_of * jnp.repeat(draws, extent[axis_at] // parts).reshape([-1 if axis == axis_at else 1 for axis in range(len(extent))])
    return factor_of


def scatter_about(own_key, extent, deviation, reach, pieces=(), held_as=jnp.bfloat16):
    result = jax.random.normal(own_key, extent, jnp.float32) * deviation
    if len(pieces) > 0:
        result = shard_levels(own_key, extent, pieces, -0.22, 0.18) * result
    return jnp.clip(result, min=-reach, max=reach).astype(held_as)


def bell_draw_with(rng, extent, scale, limit, pieces, heavy, kind=jnp.bfloat16):
    array = scale * jax.random.normal(rng, extent, jnp.float32)
    if pieces:
        array = array * shard_levels(rng, extent, pieces, -0.22, 0.18)
    return jnp.clip(strengthened(array, jax.random.fold_in(rng, 3), *heavy), -limit, limit).astype(kind)


def setup_inputs(seed: int = 0) -> dict:
    key_of = jax.random.split(jax.random.key(seed), 6)
    return {
        "tokens": scatter_about(key_of[0], (TOKENS, D), 1.0, 6.0, ((0, 256),)),
        "cotangent": scatter_about(key_of[1], (TOKENS, FF), 1.0, 6.0, ((0, 256),)),
        "pseudo_grad": bell_draw_with(key_of[2], (REPLICAS, D, FF), 1.0, 6.0, ((0, 16), (1, 16)), (0, 1, 16, 2.0)),
        "anchor": scatter_about(key_of[3], (D, FF), 1.0, 6.0, ((0, 256),), jnp.float32),
        "momentum": scatter_about(key_of[4], (D, FF), 1.0, 6.0, ((0, 256),), jnp.float32),
    }


outer_rate = 0.7
momentum_decay = 0.9

def reference(tokens, cotangent, pseudo_grad, anchor, momentum):
    mean_delta = lax.optimization_barrier(jnp.sum(pseudo_grad.astype(jnp.float32), axis=0)) / REPLICAS
    new_momentum = momentum_decay * momentum + mean_delta
    new_anchor = anchor - outer_rate * (mean_delta + momentum_decay * new_momentum)
    new_weight = new_anchor.astype(jnp.bfloat16)
    factor = D ** (-0.5)
    up_acts = (jnp.dot(tokens, new_weight, preferred_element_type=jnp.float32) * factor).astype(jnp.bfloat16)
    inputs_grouped = tokens.reshape(REPLICAS, SHARDS, TOK_DEV, D)
    grads_grouped = cotangent.reshape(REPLICAS, SHARDS, TOK_DEV, FF)

    def device_term(running, operands):
        inputs_dev, grads_dev = operands
        product = lax.dot_general(inputs_dev, grads_dev, (((0,), (0,)), ((), ())), preferred_element_type=jnp.float32) * factor
        return (running + product, None)

    def group_grad(operands):
        running, unused = lax.scan(device_term, jnp.zeros((D, FF), jnp.float32), operands)
        return running.astype(jnp.bfloat16)
    weight_grad = lax.map(group_grad, (inputs_grouped, grads_grouped))
    return (new_anchor, new_momentum, up_acts, weight_grad)
```

```python
import jax
import jax.numpy as jnp
from jax import lax
from jax.sharding import PartitionSpec as P

outer_rate = 0.7
momentum_decay = 0.9

AXES = ("replica", "shard")
f32 = jnp.float32
bf16 = jnp.bfloat16

GRAD_CHUNKS = (512, 512, 384, 384)
ACT_CHUNKS = (896, 896)


def place(x, zh, c, zl, y):
    return (((x % 4) * 2 + zh) * 2 + c) * 16 + zl * 4 + y % 4


def table(move):
    pairs = []
    for x in range(4):
        for zh in range(2):
            for c in range(2):
                for zl in range(4):
                    for y in range(4):
                        pairs.append((place(x, zh, c, zl, y), place(*move(x, zh, c, zl, y))))
    return pairs


def x_by(d):
    return table(lambda x, zh, c, zl, y: (x + d, zh, c, zl, y))


def y_by(d):
    return table(lambda x, zh, c, zl, y: (x, zh, c, zl, y + d))


def zl_by(d):
    return table(lambda x, zh, c, zl, y: (x, zh, c, (zl + d) % 4, y))


CORE = table(lambda x, zh, c, zl, y: (x, zh, 1 - c, zl, y))
ZH = table(lambda x, zh, c, zl, y: (x, 1 - zh, c, zl, y))
ZL1 = table(lambda x, zh, c, zl, y: (x, zh, c, zl ^ 1, y))
ZL2 = table(lambda x, zh, c, zl, y: (x, zh, c, zl ^ 2, y))
X_AHEAD = table(lambda x, zh, c, zl, y: (x + 1 - 2 * c, zh, c, zl, y))
X_BACK = table(lambda x, zh, c, zl, y: (x - 1 + 2 * c, zh, c, zl, y))
Y_AHEAD = table(lambda x, zh, c, zl, y: (x, zh, c, zl, y + 1 - 2 * c))
Y_BACK = table(lambda x, zh, c, zl, y: (x, zh, c, zl, y - 1 + 2 * c))


def send(array, pairs):
    return lax.ppermute(array, AXES, pairs)


def pick(array, at, axis=0):
    return lax.dynamic_index_in_dim(array, at, axis, keepdims=False)


def turn(parts, first, axis):
    twice = jnp.stack(parts + parts[:-1], axis=axis)
    return lax.dynamic_slice_in_dim(twice, (-first) % 4, 4, axis=axis)


def bounds(widths):
    at = 0
    for width in widths:
        yield slice(at, at + width)
        at += width


def on_device(tokens, cotangent, pseudo_grad, anchor, momentum):
    factor = tokens.shape[1] ** (-0.5)
    replicas = lax.axis_size("replica")
    replica, shard = lax.axis_index("replica"), lax.axis_index("shard")
    x, zh, c = replica // 4, (replica // 2) % 2, replica % 2
    zl, y = shard // 4, shard % 4
    ahead = 1 - 2 * c
    rows, ff = anchor.shape
    tok = tokens.shape[0]

    halves = tokens.reshape(tok, 2, 2, 1024)
    near = pick(halves, zl % 2, 2).reshape(tok, 2048)
    far = send(pick(halves, 1 - zl % 2, 2), ZL1).reshape(tok, 2048)
    cots, fars = [], []
    for k, cols in enumerate(bounds(GRAD_CHUNKS)):
        own = cotangent[:, cols]
        cots.append(own)
        if k >= 2:
            own, fars[k - 2] = lax.optimization_barrier((own, fars[k - 2]))
        fars.append(send(own, ZL1))

    state = jnp.stack([anchor, momentum])
    other = send(state, ZH)
    both = jnp.stack([jnp.where(zh == 0, state, other), jnp.where(zh == 0, other, state)], axis=1)
    blocks = pseudo_grad[0].reshape(4, 2, 2, rows, ff)
    total = pick(blocks, c, 2).astype(f32) + send(pick(blocks, 1 - c, 2), CORE).astype(f32)
    summed = pick(total, x)
    for d in (1, 2, 3):
        summed = summed + send(pick(total, (x + d) % 4), x_by(d))
    summed = summed + send(summed, ZH)
    mean_delta = summed / replicas
    moment_both = momentum_decay * both[1] + mean_delta
    anchor_both = both[0] - outer_rate * (mean_delta + momentum_decay * moment_both)
    moment_out, anchor_out = pick(moment_both, zh), pick(anchor_both, zh)
    weight = anchor_both.astype(bf16)

    acts = []
    for cols in bounds(ACT_CHUNKS):
        width = cols.stop - cols.start
        part = weight[:, :, cols]
        part = turn([send(part, zl_by(3)), send(part, zl_by(2)), send(part, zl_by(1)), part], zl - 3, 0)
        part = turn([send(part, y_by(1)), part, send(part, y_by(-1)), send(part, y_by(2))], y - 1, 1)
        behind = send(part, X_AHEAD)
        front = send(part, X_BACK)
        across = send(behind, X_AHEAD)
        whole = jnp.zeros((16, 4, 2, 2, rows, width), bf16)
        for piece, at, there in (
            (part, x, x),
            (behind, x - ahead, x + ahead),
            (front, x + ahead, x - ahead),
            (across, x + 2, x + 2),
        ):
            mine = piece.reshape(16, 1, 2, 1, rows, width)
            theirs = send(piece, CORE).reshape(16, 1, 2, 1, rows, width)
            whole = lax.dynamic_update_slice(whole, mine, (0, at % 4, 0, c, 0, 0))
            whole = lax.dynamic_update_slice(whole, theirs, (0, there % 4, 0, 1 - c, 0, 0))
        product = jnp.dot(tokens, whole.reshape(4096, width), preferred_element_type=f32)
        acts.append((product * factor).astype(bf16))
    up_acts = jnp.concatenate(acts, axis=1)

    grads = []
    for own, far_cot in zip(cots, fars):
        contract = (((0,), (0,)), ((), ()))
        term = lax.dot_general(near, own, contract, preferred_element_type=f32)
        term = term + lax.dot_general(far, far_cot, contract, preferred_element_type=f32)
        term = (term * factor).reshape(2, 4, 256, own.shape[1])
        first = send(pick(term, (y + 2) % 4, 1).astype(bf16), Y_AHEAD)
        back = send(pick(term, (y - ahead) % 4, 1).astype(bf16), Y_BACK)
        onward = (pick(term, (y + ahead) % 4, 1) + first.astype(f32)).astype(bf16)
        onward = send(onward, Y_AHEAD)
        ring = pick(term, y, 1) + onward.astype(f32) + back.astype(f32)
        last = send(pick(ring, 1 - zl // 2).astype(bf16), ZL2)
        grads.append((pick(ring, zl // 2) + last.astype(f32)).astype(bf16))
    weight_grad = jnp.concatenate(grads, axis=1)[None]
    return (anchor_out, moment_out, up_acts, weight_grad)


def solution(mesh):
    in_specs = (
        P(("replica", "shard"), None),
        P(("replica", "shard"), None),
        P("replica", "shard", None),
        P(("shard", "replica"), None),
        P(("shard", "replica"), None),
    )
    out_specs = (
        P(("shard", "replica"), None),
        P(("shard", "replica"), None),
        P(("replica", "shard"), None),
        P("replica", "shard", None),
    )
    return jax.shard_map(
        on_device, mesh=mesh, in_specs=in_specs, out_specs=out_specs, check_vma=False
    )
```

```python
import functools

import jax
import jax.numpy as jnp
from jax import lax
from jax.experimental import pallas as pl
from jax.experimental.pallas import tpu as pltpu
from jax.sharding import PartitionSpec as P

outer_rate = 0.7
momentum_decay = 0.9

AXES = ("replica", "shard")
f32 = jnp.float32
bf16 = jnp.bfloat16
HALF = 896
VMEM = 56 * 2**20


def place(x, zh, c, zl, y):
    return (((x % 4) * 2 + zh) * 2 + c) * 16 + zl * 4 + y % 4


def table(move):
    pairs = []
    for x in range(4):
        for zh in range(2):
            for c in range(2):
                for zl in range(4):
                    for y in range(4):
                        pairs.append((place(x, zh, c, zl, y), place(*move(x, zh, c, zl, y))))
    return pairs


def x_by(d):
    return table(lambda x, zh, c, zl, y: (x + d, zh, c, zl, y))


def y_by(d):
    return table(lambda x, zh, c, zl, y: (x, zh, c, zl, y + d))


def zl_by(d):
    return table(lambda x, zh, c, zl, y: (x, zh, c, (zl + d) % 4, y))


CORE = table(lambda x, zh, c, zl, y: (x, zh, 1 - c, zl, y))
ZH = table(lambda x, zh, c, zl, y: (x, 1 - zh, c, zl, y))
ZL1 = table(lambda x, zh, c, zl, y: (x, zh, c, zl ^ 1, y))
ZL2 = table(lambda x, zh, c, zl, y: (x, zh, c, zl ^ 2, y))
X_AHEAD = table(lambda x, zh, c, zl, y: (x + 1 - 2 * c, zh, c, zl, y))
X_BACK = table(lambda x, zh, c, zl, y: (x - 1 + 2 * c, zh, c, zl, y))
Y_AHEAD = table(lambda x, zh, c, zl, y: (x, zh, c, zl, y + 1 - 2 * c))
Y_BACK = table(lambda x, zh, c, zl, y: (x, zh, c, zl, y - 1 + 2 * c))


def send(array, pairs):
    return lax.ppermute(array, AXES, pairs)


def gate_body(*refs):
    pass


def gate(array, *first):
    return pl.pallas_call(
        gate_body,
        in_specs=[pl.BlockSpec(memory_space=pl.ANY)] * (1 + len(first)),
        out_specs=pl.BlockSpec(memory_space=pl.ANY),
        out_shape=jax.ShapeDtypeStruct(array.shape, array.dtype),
        input_output_aliases={0: 0},
        compiler_params=pltpu.CompilerParams(vmem_limit_bytes=VMEM),
        cost_estimate=pl.CostEstimate(flops=0, bytes_accessed=0, transcendentals=0),
    )(array, *first)


def pick(array, at, axis=0):
    return lax.dynamic_index_in_dim(array, at, axis, keepdims=False)


def half_of(array, at):
    return jnp.where(at == 0, array[..., :HALF], array[..., HALF:])


def by_index(at, low, high):
    return jnp.stack([jnp.where(at == 0, low, high), jnp.where(at == 0, high, low)])


def stack_body(count, at, *refs):
    out = refs[-1]
    for k, ref in enumerate(refs[:count]):
        out[:, at[k]] = ref[...]


def ring_stack(parts, at, *after):
    first, *rest = parts[0].shape
    shape = (first, len(parts), *rest)
    return pl.pallas_call(
        functools.partial(stack_body, len(parts)),
        in_specs=[pl.BlockSpec(memory_space=pltpu.SMEM)]
        + [pl.BlockSpec(memory_space=pltpu.VMEM)] * len(parts)
        + [pl.BlockSpec(memory_space=pl.ANY)] * len(after),
        out_specs=pl.BlockSpec(memory_space=pltpu.VMEM),
        out_shape=jax.ShapeDtypeStruct(shape, parts[0].dtype),
        compiler_params=pltpu.CompilerParams(vmem_limit_bytes=VMEM),
        cost_estimate=pl.CostEstimate(flops=0, bytes_accessed=0, transcendentals=0),
    )(jnp.stack(at).astype(jnp.int32) % 4, *parts, *after)


def pack_body(width, count, at, *refs):
    out = refs[-1]
    first = width[1] if width else 0
    if width:
        out[:, :first] = refs[0][...]
    for k in range(count):
        out[:, first + 256 * k : first + 256 * (k + 1)] = refs[1 + k][...]


def pack(cot, tokens, width, at, *after):
    count = at.shape[0]
    rows = tokens.shape[0]
    half = width[0] // HALF if width else 0
    columns = 256 * count + (width[1] if width else 0)
    step = rows // 2

    def block(k):
        return pl.BlockSpec((step, 256), lambda i, at: (i, at[k]))

    return pl.pallas_call(
        functools.partial(pack_body, width, count),
        grid_spec=pltpu.PrefetchScalarGridSpec(
            num_scalar_prefetch=1,
            grid=(2,),
            in_specs=[pl.BlockSpec((step, HALF if width else 128), lambda i, at: (i, half))]
            + [block(k) for k in range(count)]
            + [pl.BlockSpec(memory_space=pl.ANY)] * len(after),
            out_specs=pl.BlockSpec((step, columns), lambda i, at: (i, 0)),
        ),
        out_shape=jax.ShapeDtypeStruct((rows, columns), tokens.dtype),
        compiler_params=pltpu.CompilerParams(vmem_limit_bytes=VMEM),
        cost_estimate=pl.CostEstimate(flops=0, bytes_accessed=0, transcendentals=0),
    )(jnp.zeros((1,), jnp.int32) if count == 0 else at.astype(jnp.int32), cot, *[tokens] * count, *after)


def term_body(factor, spec, at, *refs):
    count, fars, cots = spec
    nears, refs = refs[:count], refs[count:]
    far_refs, refs = refs[:fars], refs[fars:]
    cot, far_cots, outs = refs[0], refs[1 : 1 + len(cots)], refs[-count:]
    contract = (((0,), (0,)), ((), ()))

    def add(half):
        low = cots[half]
        near = jnp.concatenate([ref[...] for ref in nears], axis=1)
        far = [ref[...] if ref.shape[1] != HALF + 512 else ref[:, HALF:] for ref in far_refs]
        far = jnp.concatenate(far, axis=1)
        far_cot = far_cots[half][:, low : low + HALF]
        total = lax.dot_general(near, cot[...], contract, preferred_element_type=f32)
        total = total + lax.dot_general(far, far_cot, contract, preferred_element_type=f32)
        for k, out in enumerate(outs):
            out[...] = (total[256 * k : 256 * (k + 1)] * factor).astype(out.dtype)

    for half in range(len(cots)):
        pl.when(pl.program_id(0) == half)(functools.partial(add, half))


def terms(at, tokens, fars, cotangent, half, far_cots, factor, kinds, *after):
    tok = tokens.shape[0]
    count, halves = len(kinds), len(far_cots)

    def near(k):
        return pl.BlockSpec((tok, 256), lambda h, at: (0, at[k]))

    def far(first, columns):
        return pl.BlockSpec((tok, columns), lambda h, at: (0, first // columns))

    return pl.pallas_call(
        functools.partial(term_body, factor, (count, len(fars), tuple(low for _, low in far_cots))),
        grid_spec=pltpu.PrefetchScalarGridSpec(
            num_scalar_prefetch=1,
            grid=(halves,),
            in_specs=[near(k) for k in range(count)]
            + [far(first, columns) for _, first, columns in fars]
            + [pl.BlockSpec((tok, HALF), lambda h, at: (0, half + h))]
            + [pl.BlockSpec(array.shape, lambda h, at: (0, 0)) for array, _ in far_cots]
            + [pl.BlockSpec(memory_space=pl.ANY)] * len(after),
            out_specs=[pl.BlockSpec((256, HALF), lambda h, at: (0, h))] * count,
        ),
        out_shape=[jax.ShapeDtypeStruct((256, HALF * halves), kind) for kind in kinds],
        compiler_params=pltpu.CompilerParams(vmem_limit_bytes=VMEM),
        cost_estimate=pl.CostEstimate(flops=0, bytes_accessed=0, transcendentals=0),
    )(
        at.astype(jnp.int32),
        *[tokens] * count,
        *[array for array, _, _ in fars],
        cotangent,
        *[array for array, _ in far_cots],
        *after,
    )


def act_body(factor, at, mine, other, *refs):
    pieces, (out_mine, out_other, block, sum_mine, sum_other) = refs[:4], refs[-5:]
    step = pl.program_id(0)
    shards = block.shape[0]
    for k, piece in enumerate(pieces):
        block[:, at[k]] = piece[...].reshape(shards, 64, HALF)
    held = block[...].reshape(shards * 256, HALF)
    for tokens, total, out in ((mine, sum_mine, out_mine), (other, sum_other, out_other)):
        part = jnp.dot(tokens[...], held, preferred_element_type=f32)

        @pl.when(step == 0)
        def _(total=total, part=part):
            total[...] = part

        @pl.when(step > 0)
        def _(total=total, part=part):
            total[...] += part

        @pl.when(step == pl.num_programs(0) - 1)
        def _(total=total, out=out):
            out[...] = (total[...] * factor).astype(out.dtype)


def activations(mine, other, pieces, at, factor, *after):
    tok, depth = mine.shape
    shards = 4
    rows = pl.BlockSpec((tok, shards * 256), lambda i, at: (0, i))
    piece = pl.BlockSpec((shards * 64, HALF), lambda i, at: (i, 0))
    whole = pl.BlockSpec((tok, HALF), lambda i, at: (0, 0))
    return pl.pallas_call(
        functools.partial(act_body, factor),
        grid_spec=pltpu.PrefetchScalarGridSpec(
            num_scalar_prefetch=1,
            grid=(depth // (shards * 256),),
            in_specs=[rows, rows] + [piece] * 4 + [pl.BlockSpec(memory_space=pl.ANY)] * len(after),
            out_specs=[whole, whole],
            scratch_shapes=[
                pltpu.VMEM((shards, 4, 64, HALF), bf16),
                pltpu.VMEM((tok, HALF), f32),
                pltpu.VMEM((tok, HALF), f32),
            ],
        ),
        out_shape=[jax.ShapeDtypeStruct((tok, HALF), bf16)] * 2,
        compiler_params=pltpu.CompilerParams(vmem_limit_bytes=VMEM),
        cost_estimate=pl.CostEstimate(flops=0, bytes_accessed=0, transcendentals=0),
    )(jnp.stack(at).astype(jnp.int32) % 4, mine, other, *pieces, *after)


def on_device(tokens, cotangent, pseudo_grad, anchor, momentum):
    factor = tokens.shape[1] ** (-0.5)
    replicas = lax.axis_size("replica")
    replica, shard = lax.axis_index("replica"), lax.axis_index("shard")
    x, zh, c = replica // 4, (replica // 2) % 2, replica % 2
    zl, y = shard // 4, shard % 4
    ahead = 1 - 2 * c
    rows, ff = anchor.shape

    early = jnp.stack([(y + 2) % 4, (y - ahead) % 4])
    late = jnp.stack([(y + ahead) % 4, y])
    both = jnp.concatenate([early, late])
    pass_on, keep = (zl ^ 2) * 4, zl * 4

    blocks = pseudo_grad[0].reshape(4, 4 * rows, ff)
    from_core = send(half_of(blocks, 1 - c), CORE)
    base = anchor - (outer_rate * momentum_decay * momentum_decay) * momentum
    base_core = send(half_of(base, 1 - c), CORE)
    base = by_index(c, half_of(base, c), base_core)

    no_blocks = jnp.zeros((0,), jnp.int32)
    far_f1 = send(pack(cotangent, tokens, None, (3 - zl) * 4 + early), ZL1)

    total = half_of(blocks, c).astype(f32) + from_core.astype(f32)
    got = [send(pick(total, (x + d) % 4).astype(bf16), x_by(d)) for d in (1, 2, 3)]
    total = pick(total, x)
    for part in got:
        total = total + part.astype(f32)
    total = total.reshape(2, 2, rows, HALF)
    got = send(gate(pick(total, 1 - zh).astype(bf16), far_f1), ZH)
    mean_delta = (pick(total, zh) + got.astype(f32)) / replicas
    weight = base - (outer_rate * (1 + momentum_decay)) * mean_delta
    weight = weight.astype(bf16)
    weight = by_index(zh, weight, send(weight, ZH)).reshape(4 * rows, HALF)

    got = [send(weight, zl_by(d)) for d in (1, 2, 3)]
    weight = ring_stack([weight[None], *[g[None] for g in got]], [zl, zl - 1, zl - 2, zl - 3])[0]
    other_tokens = send(tokens, CORE)
    z_2_in = pack(cotangent, tokens, (0, HALF), (3 - zl) * 4 + late, weight)
    z_2 = send(z_2_in, ZL1)
    got = [send(weight, y_by(d)) for d in (2, 1, -1)]
    weight = ring_stack([weight, *got], [y, y - 2, y - 1, y + 1]).reshape(1024, HALF)
    xa = send(weight, X_AHEAD)
    xb = send(weight, X_BACK)
    cot_1 = send(pack(cotangent, tokens, (HALF, HALF), no_blocks, weight), ZL1)
    far_o = send(pack(cotangent, tokens, None, (zl ^ 1) * 4 + both, weight), ZL1)
    xr_in = gate(xa, xb)
    xr = send(xr_in, X_AHEAD)

    delta_core = send(pick(mean_delta, 1 - c), CORE)
    delta = by_index(c, pick(mean_delta, c), delta_core)
    delta = jnp.concatenate([delta[0], delta[1]], axis=1)
    moment_out = momentum_decay * momentum + delta
    anchor_out = anchor - outer_rate * (delta + momentum_decay * moment_out)

    def ring_sum(block, got):
        return block + got.astype(f32)

    kinds = (bf16, bf16, f32, f32)
    first, second = (far_f1, 0, 512), (z_2, 0, HALF + 512)
    f_0 = terms(pass_on + both, tokens, [first, second], cotangent, 0, [(z_2, 0)], factor, kinds, weight)
    u_a = send(f_0[0], Y_AHEAD)
    u_b = send(f_0[1], Y_BACK)
    u_c = send(ring_sum(f_0[2], u_a).astype(bf16), Y_AHEAD)
    last_0 = send(ring_sum(ring_sum(f_0[3], u_b), u_c).astype(bf16), ZL2)
    f_1 = terms(pass_on + both, tokens, [first, second], cotangent, 1, [(cot_1, 0)], factor, kinds, f_0[3])
    v_a = send(f_1[0], Y_AHEAD)
    v_b = send(f_1[1], Y_BACK)
    v_c = send(ring_sum(f_1[2], v_a).astype(bf16), Y_AHEAD)
    last_1 = send(ring_sum(ring_sum(f_1[3], v_b), v_c).astype(bf16), ZL2)
    cots = [(z_2, 0), (cot_1, 0)]
    o = terms(keep + both, tokens, [(far_o, 0, 1024)], cotangent, 0, cots, factor, kinds, f_1[3], xr_in)
    w_a = send(o[0], Y_AHEAD)
    w_b = send(o[1], Y_BACK)
    w_c = send(gate(ring_sum(o[2], w_a).astype(bf16), last_0), Y_AHEAD)

    act, back = activations(
        tokens, other_tokens, [weight, xr_in, xb, xr], [x, x - ahead, x + ahead, x + 2], factor, o[3]
    )
    back = send(back, CORE)
    up_acts = jnp.where(
        c == 0, jnp.concatenate([act, back], axis=1), jnp.concatenate([back, act], axis=1)
    )
    grad = ring_sum(ring_sum(o[3], w_b), w_c)
    grad = ring_sum(grad, jnp.concatenate([last_0, last_1], axis=1))
    return (anchor_out, moment_out, up_acts, grad.astype(bf16)[None])


def solution(mesh):
    in_specs = (
        P(("replica", "shard"), None),
        P(("replica", "shard"), None),
        P("replica", "shard", None),
        P(("shard", "replica"), None),
        P(("shard", "replica"), None),
    )
    out_specs = (
        P(("shard", "replica"), None),
        P(("shard", "replica"), None),
        P(("replica", "shard"), None),
        P("replica", "shard", None),
    )
    return jax.shard_map(
        on_device, mesh=mesh, in_specs=in_specs, out_specs=out_specs, check_vma=False
    )
```
